32 devices in a mesh: ctx: 8 (over y, x, core), kvh: 4 (over z).
Axes of the slice: x: 2, y: 2, z: 4, core: 2. Of those that a mesh axis runs over, the one named last changes fastest.
Arguments:
- x_kv: bfloat16 [2048, 3072], P('ctx'), may hold values from -17 to 17, as said below
- w_kv: bfloat16 [3072, 2048], P(None, 'kvh'), may hold values from -0.0546875 to 0.0546875
- queries: bfloat16 [3, 3072, 3072], P(None, 'ctx', 'kvh'), may hold values from -6 to 6
- d_out: bfloat16 [3, 3072, 3072], P(None, 'ctx', 'kvh'), may hold values from -12 to 12
- lse: float32 [3, 3072, 24], P(None, 'ctx', 'kvh'), may hold values from 7 to 10
- delta: float32 [3, 3072, 24], P(None, 'ctx', 'kvh'), may hold values from -24 to 24
- offsets: int32 [8], P('ctx'), may hold values from 1 to 2047
- block_mask: int32 [24, 16], P('ctx'), may hold values 0 or 1
Outputs:
- d_queries: bfloat16 [3, 3072, 3072], P(None, 'ctx', 'kvh')
- d_x: bfloat16 [2048, 3072], P('ctx', 'kvh')
- d_w: float32 [3072, 2048], P('ctx', 'kvh')
The draws below stay inside these ranges and needn't reach their ends.
Inputs may be any that keep to these rules, and one draw needn't show every extreme that they name: `x_kv`: feature scales differ from column to column.
All inputs are finite; a program needn't handle non-finite values.
Results may differ from the reference program's by a relative error of at most 0.012.
Values may be sent and summed in bfloat16 or wider, within the bound.
A program may use at most 64 MiB of HBM per device.

```python
import jax
import jax.numpy as jnp
from jax import lax

D = 3072
H = 24
KVH = 8
HD = 128
NL = 3
QBLK = 128
KBLK = 128
Q_DEV = 384
QUERIES = 3072
S_KV = 2048
GROUP = 3
CTX_SHARDS = 8


def draw_x_kv(key, part):
    first, second = jax.random.split(jax.random.fold_in(key, 71))
    ramp = jnp.arange(D, dtype=jnp.float32) / D
    jitter = jax.random.uniform(first, (D,), jnp.float32, 0.0, 0.25)
    base = jnp.clip(jax.random.normal(second, (S_KV, D), jnp.float32), -6.0, 6.0)
    scale = 10.0 ** (0.5 * ramp + jitter)
    return (base * scale[None, :] * 0.5).astype(jnp.bfloat16)


def place_ends(values, rng, low, top_value):
    dims = values.shape
    place = [jax.random.randint(jax.random.fold_in(rng, axis), (), 0, dims[axis]) for axis in range(len(dims))]
    values = values.at[tuple(place)].set(low)
    longest = dims.index(max(dims))
    place[longest] = (place[longest] + 1) % dims[longest]
    return values.at[tuple(place)].set(top_value)


def shard_levels(stream_key, dims, shards, least, top_value):
    def one(axis_at, parts):
        heights = jax.random.uniform(jax.random.fold_in(jax.random.fold_in(stream_key, 6), axis_at), (parts,), jnp.float32, least / len(shards), top_value / len(shards))
        return jnp.repeat(jnp.exp(heights), dims[axis_at] // parts).reshape((-1,) + (1,) * (len(dims) - axis_at - 1))

    level = one(*shards[0])
    for cut in shards[1:]:
        level = level * one(*cut)
    return level


def bell_draw(own_key, dims, spread, reach, pieces=(), kind=jnp.bfloat16):
    entries = jax.random.normal(own_key, dims, jnp.float32) * spread
    if len(pieces) > 0:
        entries = shard_levels(own_key, dims, pieces, -0.22, 0.18) * entries
    return jnp.clip(entries, min=-reach, max=reach).astype(kind)


def setup_inputs(seed: int = 0) -> dict:
    key_of = jax.random.split(jax.random.key(seed), 9)
    return {
        "x_kv": draw_x_kv(jax.random.fold_in(key_of[8], 71), 0),
        "w_kv": bell_draw(key_of[1], (D, KVH * 2 * HD), (4 * D) ** -0.5, 0.0546875, ((1, 4),)),
        "queries": bell_draw(key_of[2], (NL, QUERIES, H * HD), 1.0, 6.0, ((1, 8), (2, 4))),
        "d_out": bell_draw(key_of[3], (NL, QUERIES, H * HD), 2.0, 12.0, ((1, 8), (2, 4))),
        "lse": jnp.clip(7.0 + 3.0 * jax.random.uniform(key_of[4], (NL, QUERIES, H), jnp.float32) ** shard_levels(key_of[4], (NL, QUERIES, H), ((1, 8), (2, 4)), -0.2, 0.2), 7.0, 10.0),
        "delta": bell_draw(key_of[5], (NL, QUERIES, H), 4.0, 24.0, ((1, 8), (2, 4)), jnp.float32),
        "offsets": place_ends(jax.random.randint(key_of[6], (CTX_SHARDS,), 1, S_KV), jax.random.fold_in(key_of[6], 1), 1, S_KV - 1).astype(jnp.int32),
        "block_mask": place_ends((jax.random.randint(key_of[7], (QUERIES // QBLK, S_KV // KBLK), 0, 4) < 3).astype(jnp.int32), jax.random.fold_in(key_of[7], 1), 0, 1),
    }


def reference(x_kv, w_kv, queries, d_out, lse, delta, offsets, block_mask):
    kv = jnp.dot(x_kv, w_kv, preferred_element_type=jnp.float32).astype(jnp.bfloat16)
    key_value_four = kv.astype(jnp.float32).reshape(S_KV, KVH, 2, HD)
    kmat = key_value_four[:, :, 0, :]
    value_matrix = key_value_four[:, :, 1, :]
    nblocks = QUERIES // QBLK
    keys = jnp.arange(S_KV, dtype=jnp.int32)
    scale = HD ** (-0.5)
    q_blocks = jnp.transpose(queries.reshape(NL, nblocks, QBLK, KVH, GROUP, HD), (1, 0, 2, 3, 4, 5))
    o_blocks = jnp.transpose(d_out.reshape(NL, nblocks, QBLK, KVH, GROUP, HD), (1, 0, 2, 3, 4, 5))
    lse_blocks = jnp.transpose(lse.reshape(NL, nblocks, QBLK, KVH, GROUP), (1, 0, 3, 4, 2))
    delta_blocks = jnp.transpose(delta.reshape(NL, nblocks, QBLK, KVH, GROUP), (1, 0, 3, 4, 2))
    block_ids = jnp.arange(nblocks, dtype=jnp.int32)

    def step_block(carry, inputs):
        dk_sum, dv_sum = carry
        q_block, o_block, lse_block, delta_block, index = inputs
        rows = index * QBLK + jnp.arange(QBLK, dtype=jnp.int32)
        limit = offsets[rows // Q_DEV] + rows % Q_DEV
        allowed = block_mask[index][keys // KBLK]
        visible = (allowed == 1)[None, :] & (keys[None, :] < limit[:, None])
        dq_layers = []
        for layer_index in range(NL):
            qmat = q_block[layer_index].astype(jnp.float32)
            output_matrix = o_block[layer_index].astype(jnp.float32)
            scores = jnp.einsum('qkgd,nkd->kgqn', qmat, kmat) * scale
            probs = jnp.where(visible[None, None], jnp.exp(scores - lse_block[layer_index][..., None]), jnp.float32(0.0))
            p_half = probs.astype(jnp.bfloat16).astype(jnp.float32)
            probability_gradient = jnp.einsum('qkgd,nkd->kgqn', output_matrix, value_matrix)
            dscore = (probs * (probability_gradient - delta_block[layer_index][..., None])).astype(jnp.bfloat16).astype(jnp.float32)
            dv_sum = dv_sum + jnp.einsum('kgqn,qkgd->nkd', p_half, output_matrix)
            dk_sum = dk_sum + jnp.einsum('kgqn,qkgd->nkd', dscore, qmat) * scale
            dq_layers.append((jnp.einsum('kgqn,nkd->qkgd', dscore, kmat) * scale).astype(jnp.bfloat16))
        return ((dk_sum, dv_sum), jnp.stack(dq_layers, axis=0))
    init = (jnp.zeros((S_KV, KVH, HD), jnp.float32), jnp.zeros((S_KV, KVH, HD), jnp.float32))
    (dk_sum, dv_sum), dq_all = lax.scan(step_block, init, (q_blocks, o_blocks, lse_blocks, delta_blocks, block_ids))
    d_queries = jnp.transpose(dq_all, (1, 0, 2, 3, 4, 5)).reshape(NL, QUERIES, H * HD)
    dkv = jnp.stack([dk_sum, dv_sum], axis=2).reshape(S_KV, KVH * 2 * HD)
    dkv_half = dkv.astype(jnp.bfloat16)
    d_x = jnp.dot(dkv_half, w_kv.T, preferred_element_type=jnp.float32).astype(jnp.bfloat16)
    grad = jnp.dot(x_kv.T, dkv_half, preferred_element_type=jnp.float32)
    msq = jnp.mean(grad * grad)
    d_w = grad / jnp.sqrt(msq + 1e-06)
    return (d_queries, d_x, d_w)
```

```python
import functools
import math

import jax
import jax.numpy as jnp
from jax import lax
from jax.experimental import pallas as pl
from jax.experimental.pallas import tpu as pltpu
from jax.sharding import PartitionSpec as P

D = 3072
KVH = 8
HD = 128
QBLK = 128
KBLK = 128

NT = (((1,), (1,)), ((), ()))
NN = (((1,), (0,)), ((), ()))
TN = (((0,), (0,)), ((), ()))
F32 = jnp.float32
BF16 = jnp.bfloat16


def dot(a, b, dims):
    return lax.dot_general(a, b, dims, preferred_element_type=F32)


def kernel(
    dims,
    x_ref,
    xs_ref,
    w_ref,
    q_ref,
    o_ref,
    lse_ref,
    delta_ref,
    mask_ref,
    lim_ref,
    dq_ref,
    dx_ref,
    dw_ref,
    kvw,
    xall,
    wall,
    snd,
    rcv,
    dkvc,
    dkvz,
    qt,
    ot,
    dqacc,
    bias,
    acc,
    sqc,
    sqz,
    kv_s,
    kv_r,
    x_s,
    x_r,
    w_s,
    w_r,
    p_s,
    p_r,
    c_s,
    c_r,
    z_s,
    z_r,
    sc_s,
    sc_r,
    sz_s,
    sz_r,
    loc,
):
    C, Z, kvd, G, L, nq, own, total = dims
    me = lax.axis_index("ctx")
    mz = lax.axis_index("kvh")
    cw = xall.shape[2]
    zw = wall.shape[1]
    scale = HD ** (-0.5)
    c2 = scale * math.log2(math.e)
    sliced = cw % 128 == 0
    kper = own // KBLK

    def ctx_copy(src, dst, ss, rs, dev):
        return pltpu.make_async_remote_copy(
            src_ref=src, dst_ref=dst, send_sem=ss, recv_sem=rs,
            device_id={"ctx": dev}, device_id_type=pl.DeviceIdType.MESH)

    def z_copy(src, dst, ss, rs, dev):
        return pltpu.make_async_remote_copy(
            src_ref=src, dst_ref=dst, send_sem=ss, recv_sem=rs,
            device_id={"kvh": dev}, device_id_type=pl.DeviceIdType.MESH)

    def each(n, mine, f, back=False):
        def one(j, carry):
            f(lax.rem(mine + (n - j if back else j), n))
            return carry

        lax.fori_loop(1, n, one, 0)

    def x_cols(d):
        if sliced:
            return x_ref.at[:, pl.ds(pl.multiple_of(d * cw, 128), cw)]
        return xs_ref.at[d]

    def w_rows(d):
        return w_ref.at[pl.ds(pl.multiple_of(d * zw, 128), zw), :]

    def kv_copy(h, d, slot):
        return ctx_copy(kvw.at[h, slot], kvw.at[h, slot], kv_s.at[h, d], kv_r.at[h, slot], d)

    def x_copy(d, slot):
        return ctx_copy(x_cols(d), xall.at[slot], x_s.at[d], x_r.at[slot], d)

    def w_copy(d, slot):
        return z_copy(w_rows(d), wall.at[slot], w_s.at[d], w_r.at[slot], d)

    def p_copy(h, d, slot):
        return ctx_copy(snd.at[h, d], rcv.at[h, slot], p_s.at[h, d], p_r.at[h, slot], d)

    def c_copy(h, d, slot):
        return ctx_copy(dkvc.at[h, slot], dkvc.at[h, slot], c_s.at[h, d], c_r.at[h, slot], d)

    def z_half(h, d, slot):
        return z_copy(dkvz.at[h, slot], dkvz.at[h, slot], z_s.at[h, d], z_r.at[h, slot], d)

    def sc_copy(d, slot):
        return ctx_copy(sqc.at[slot], sqc.at[slot], sc_s.at[d], sc_r.at[slot], d)

    def sz_copy(d, slot):
        return z_copy(sqz.at[slot], sqz.at[slot], sz_s.at[d], sz_r.at[slot], d)

    barrier = pltpu.get_barrier_semaphore()
    each(C, me, lambda d: pl.semaphore_signal(
        barrier, inc=1, device_id={"ctx": d}, device_id_type=pl.DeviceIdType.MESH))
    each(Z, mz, lambda d: pl.semaphore_signal(
        barrier, inc=1, device_id={"kvh": d}, device_id_type=pl.DeviceIdType.MESH))
    own_x = pltpu.make_async_copy(x_cols(me), xall.at[me], loc.at[0])
    own_w = pltpu.make_async_copy(w_rows(mz), wall.at[mz], loc.at[1])
    own_x.start()
    own_w.start()

    for h in range(kvd):
        cols = slice(h * 2 * HD, (h + 1) * 2 * HD)
        kvw[h, me] = dot(x_ref[...], w_ref[:, cols], NN).astype(BF16)
        if h == 0:
            pl.semaphore_wait(barrier, C + Z - 2)
        each(C, me, lambda d: kv_copy(h, d, me).start(), back=True)
    each(Z, mz, lambda d: w_copy(d, mz).start())
    each(C, me, lambda d: x_copy(d, me).start())

    def reduce(h):
        def add(j, total_sum):
            d = lax.rem(me + j, C)
            p_copy(h, d, d).wait_recv()
            return total_sum + rcv[h, d].astype(F32)

        half = lax.fori_loop(1, C, add, snd[h, me].astype(F32)).astype(BF16)
        dkvc[h, me] = half
        dkvz[h, mz] = half
        each(Z, mz, lambda d: z_half(h, d, mz).start())
        each(C, me, lambda d: c_copy(h, d, me).start())

    dqacc[...] = jnp.zeros_like(dqacc)
    for h in range(kvd):

        def turn(l, carry):
            for g in range(G):
                hh = h * G + g
                cols = slice(hh * HD, (hh + 1) * HD)
                qt[l, g] = jnp.transpose(q_ref[l, :, cols])
                ot[l, g] = jnp.transpose(o_ref[l, :, cols])
            return carry

        lax.fori_loop(0, L, turn, 0)
        shift = 1 if (h == kvd - 1 and h > 0) else 0

        def step(s, carry):
            owner = lax.rem(me + s + shift, C)

            @pl.when(owner != me)
            def _():
                kv_copy(h, owner, owner).wait_recv()

            kmat = kvw[h, owner, :, :HD]
            vmat = kvw[h, owner, :, HD:]
            for kb in range(kper):
                rows = mask_ref[owner * kper + kb]
                at = owner * own + kb * KBLK
                pos = at + lax.broadcasted_iota(jnp.int32, (nq, KBLK), 1)
                bias[:, kb * KBLK:(kb + 1) * KBLK] = jnp.where(
                    pos < lim_ref[...], rows, -jnp.inf)
            acc[...] = jnp.zeros_like(acc)

            def layer(l, carry):
                for g in range(G):
                    hh = h * G + g
                    cols = slice(hh * HD, (hh + 1) * HD)
                    q = q_ref[l, :, cols]
                    o = o_ref[l, :, cols]
                    sc = dot(q, kmat, NT)
                    pr = jnp.exp2(sc * c2 - lse_ref[l, :, hh:hh + 1] + bias[...])
                    dp = dot(o, vmat, NT)
                    ds = (pr * (dp - delta_ref[l, :, hh:hh + 1])).astype(BF16)
                    ph = pr.astype(BF16)
                    dqacc[l, hh] += dot(ds, kmat, NN)
                    acc[0] += dot(qt[l, g], ds, NN)
                    acc[1] += dot(ot[l, g], ph, NN)
                return carry

            lax.fori_loop(0, L, layer, 0)
            snd[h, owner, :, :HD] = jnp.transpose(acc[0] * scale).astype(BF16)
            snd[h, owner, :, HD:] = jnp.transpose(acc[1]).astype(BF16)

            @pl.when(owner != me)
            def _():
                p_copy(h, owner, me).start()

            if h > 0:

                @pl.when(s == min(1, C - 1))
                def _():
                    reduce(h - 1)

            return carry

        lax.fori_loop(0, C, step, 0)

    reduce(kvd - 1)

    def finish(l, carry):
        for hh in range(kvd * G):
            dq_ref[l, :, hh * HD:(hh + 1) * HD] = (dqacc[l, hh] * scale).astype(BF16)
        return carry

    lax.fori_loop(0, L, finish, 0)
    own_x.wait()
    own_w.wait()
    each(C, me, lambda d: x_copy(d, d).wait_recv())
    each(Z, mz, lambda d: w_copy(d, d).wait_recv())

    for h in range(kvd):
        cols = slice(h * 2 * HD, (h + 1) * 2 * HD)

        def grad(j, tot):
            d = lax.rem(me + j, C)

            @pl.when(j > 0)
            def _():
                c_copy(h, d, d).wait_recv()

            return tot + dot(xall[d], dkvc[h, d], TN)

        dw_ref[:, cols] = lax.fori_loop(0, C, grad, jnp.zeros((cw, 2 * HD), F32))
    g = dw_ref[...]
    sqc[me] = jnp.broadcast_to(jnp.sum(g * g, axis=(0, 1), keepdims=True), sqc.shape[1:])
    each(C, me, lambda d: sc_copy(d, me).start())

    dx = jnp.zeros(dx_ref.shape, F32)
    for h in range(kvd):
        cols = slice(h * 2 * HD, (h + 1) * 2 * HD)

        def part(j, tot):
            d = lax.rem(mz + j, Z)

            @pl.when(j > 0)
            def _():
                z_half(h, d, d).wait_recv()

            return tot + dot(dkvz[h, d], wall[d, :, cols], NT)

        dx = lax.fori_loop(0, Z, part, dx)
        if h == 0:
            each(C, me, lambda d: sc_copy(d, d).wait_recv())
            sqz[mz] = jnp.sum(sqc[...], axis=0)
            each(Z, mz, lambda d: sz_copy(d, mz).start())
    dx_ref[...] = dx.astype(BF16)

    each(Z, mz, lambda d: sz_copy(d, d).wait_recv())
    msq = jnp.sum(sqz[...], axis=0)[:1, :1] / total
    inv = 1.0 / jnp.sqrt(msq + 1e-6)
    dw_ref[...] = dw_ref[...] * inv

    def drain_ctx(d):
        for h in range(kvd):
            kv_copy(h, d, me).wait_send()
            p_copy(h, d, me).wait_send()
            c_copy(h, d, me).wait_send()
        x_copy(d, me).wait_send()
        sc_copy(d, me).wait_send()

    def drain_z(d):
        for h in range(kvd):
            z_half(h, d, mz).wait_send()
        w_copy(d, mz).wait_send()
        sz_copy(d, mz).wait_send()

    each(C, me, drain_ctx)
    each(Z, mz, drain_z)


def body(x_kv, w_kv, queries, d_out, lse, delta, offsets, block_mask):
    L, nq, width = queries.shape
    C, Z = lax.axis_size("ctx"), lax.axis_size("kvh")
    own, dm = x_kv.shape
    kvd = w_kv.shape[1] // (2 * HD)
    heads = width // HD
    G = heads // kvd
    cw, zw = dm // C, dm // Z
    qblocks, kblocks = block_mask.shape
    rows = jnp.transpose(jnp.where(block_mask == 1, 0.0, -jnp.inf).astype(F32))
    mask = jnp.broadcast_to(rows[:, :, None, None], (kblocks, qblocks, nq // qblocks, 1))
    mask = mask.reshape(kblocks, nq, 1)
    lim = (offsets[0] + jnp.arange(nq, dtype=jnp.int32))[:, None]
    if cw % 128 == 0:
        xs = jnp.zeros((8, 128), BF16)
    else:
        xs = jnp.transpose(x_kv.reshape(own, C, cw), (1, 0, 2))
    total = float(dm) * Z * kvd * 2 * HD
    dims = (C, Z, kvd, G, L, nq, own, total)
    vm = pl.BlockSpec(memory_space=pltpu.VMEM)
    blk = (own, 2 * HD)
    dma = pltpu.SemaphoreType.DMA
    flops = 2 * L * heads * nq * own * C * HD * 5
    return pl.pallas_call(
        functools.partial(kernel, dims),
        out_shape=(
            jax.ShapeDtypeStruct(queries.shape, BF16),
            jax.ShapeDtypeStruct((own, zw), BF16),
            jax.ShapeDtypeStruct((cw, kvd * 2 * HD), F32),
        ),
        in_specs=[vm] * 9,
        out_specs=(vm, vm, vm),
        scratch_shapes=[
            pltpu.VMEM((kvd, C) + blk, BF16),
            pltpu.VMEM((C, own, cw), BF16),
            pltpu.VMEM((Z, zw, kvd * 2 * HD), BF16),
            pltpu.VMEM((kvd, C) + blk, BF16),
            pltpu.VMEM((kvd, C) + blk, BF16),
            pltpu.VMEM((kvd, C) + blk, BF16),
            pltpu.VMEM((kvd, Z) + blk, BF16),
            pltpu.VMEM((L, G, HD, nq), BF16),
            pltpu.VMEM((L, G, HD, nq), BF16),
            pltpu.VMEM((L, heads, nq, HD), F32),
            pltpu.VMEM((nq, own), F32),
            pltpu.VMEM((2, HD, own), F32),
            pltpu.VMEM((C, 8, 128), F32),
            pltpu.VMEM((Z, 8, 128), F32),
            dma((kvd, C)), dma((kvd, C)),
            dma((C,)), dma((C,)),
            dma((Z,)), dma((Z,)),
            dma((kvd, C)), dma((kvd, C)),
            dma((kvd, C)), dma((kvd, C)),
            dma((kvd, Z)), dma((kvd, Z)),
            dma((C,)), dma((C,)),
            dma((Z,)), dma((Z,)),
            dma((2,)),
        ],
        compiler_params=pltpu.CompilerParams(
            collective_id=0, has_side_effects=True, vmem_limit_bytes=60 * 1024 * 1024
        ),
        cost_estimate=pl.CostEstimate(flops=flops, bytes_accessed=1 << 24, transcendentals=0),
    )(x_kv, xs, w_kv, queries, d_out, lse * math.log2(math.e), delta, mask, lim)


def solution(mesh):
    in_specs = (
        P("ctx", None),
        P(None, "kvh"),
        P(None, "ctx", "kvh"),
        P(None, "ctx", "kvh"),
        P(None, "ctx", "kvh"),
        P(None, "ctx", "kvh"),
        P("ctx"),
        P("ctx", None),
    )
    out_specs = (P(None, "ctx", "kvh"), P("ctx", "kvh"), P("ctx", "kvh"))
    return jax.shard_map(body, mesh=mesh, in_specs=in_specs, out_specs=out_specs, check_vma=False)
```

```python
import functools
import math

import jax
import jax.numpy as jnp
from jax import lax
from jax.experimental import pallas as pl
from jax.experimental.pallas import tpu as pltpu
from jax.sharding import PartitionSpec as P

D = 3072
KVH = 8
HD = 128
QBLK = 128
KBLK = 128

NT = (((1,), (1,)), ((), ()))
NN = (((1,), (0,)), ((), ()))
TN = (((0,), (0,)), ((), ()))
F32 = jnp.float32
BF16 = jnp.bfloat16


def dot(a, b, dims):
    return lax.dot_general(a, b, dims, preferred_element_type=F32)


def kernel(
    dims,
    x_ref,
    xs_ref,
    w_ref,
    q_ref,
    o_ref,
    lse_ref,
    delta_ref,
    mask_ref,
    off_ref,
    dq_ref,
    dx_ref,
    dw_ref,
    kvw,
    xall,
    wall,
    snd,
    prt,
    rcv,
    dkvc,
    dkvz,
    qt,
    ot,
    lse2,
    dqacc,
    bias,
    acc,
    sqc,
    sqz,
    kv_s,
    kv_f,
    kv_r,
    x_s,
    x_r,
    w_s,
    w_r,
    wf_s,
    wf_r,
    pp_s,
    pp_r,
    p_s,
    p_r,
    c_s,
    c_f,
    c_r,
    z_s,
    z_r,
    sc_s,
    sc_r,
    sz_s,
    sz_r,
    loc,
):
    C, Z, kvd, G, L, nq, own, total = dims
    me = lax.axis_index("ctx")
    mz = lax.axis_index("kvh")
    cw = xall.shape[2]
    zw = wall.shape[2] * 2
    chips = C // 2
    chip, core = me // 2, lax.rem(me, 2)
    mate = chip * 2 + 1 - core
    hw = zw // 2
    scale = HD ** (-0.5)
    c2 = scale * math.log2(math.e)
    sliced = cw % 128 == 0
    kper = own // KBLK

    def ctx_copy(src, dst, ss, rs, dev):
        return pltpu.make_async_remote_copy(
            src_ref=src, dst_ref=dst, send_sem=ss, recv_sem=rs,
            device_id={"ctx": dev}, device_id_type=pl.DeviceIdType.MESH)

    def z_copy(src, dst, ss, rs, dev):
        return pltpu.make_async_remote_copy(
            src_ref=src, dst_ref=dst, send_sem=ss, recv_sem=rs,
            device_id={"kvh": dev}, device_id_type=pl.DeviceIdType.MESH)

    def each(n, mine, f, back=False):
        def one(j, carry):
            f(lax.rem(mine + (n - j if back else j), n))
            return carry

        lax.fori_loop(1, n, one, 0)

    def x_cols(d):
        if sliced:
            return x_ref.at[:, pl.ds(pl.multiple_of(d * cw, 128), cw)]
        return xs_ref.at[d]

    def w_rows(d):
        return w_ref.at[pl.ds(pl.multiple_of(d * zw + core * hw, 64), hw), :]

    def same_core(t):
        return t * 2 + core

    def kv_copy(h, d):
        return ctx_copy(kvw.at[h, me], kvw.at[h, me], kv_s.at[h, d], kv_r.at[h, me], d)

    def kv_pass(h, t):
        k = same_core(t)
        return ctx_copy(kvw.at[h, k], kvw.at[h, k], kv_f.at[h, t], kv_r.at[h, k], mate)

    def kv_wait(h, k):
        ctx_copy(kvw.at[h, k], kvw.at[h, k], kv_s.at[h, k], kv_r.at[h, k], mate).wait_recv()

    def x_copy(d, slot):
        return ctx_copy(x_cols(d), xall.at[slot], x_s.at[d], x_r.at[slot], d)

    def w_copy(d, slot):
        return z_copy(w_rows(d), wall.at[slot, core], w_s.at[d], w_r.at[slot], d)

    def w_pass(d, part):
        return ctx_copy(wall.at[d, part], wall.at[d, part], wf_s.at[d], wf_r.at[d], mate)

    def pp_copy(h, t):
        return ctx_copy(snd.at[h, t * 2 + 1 - core], prt.at[h, t], pp_s.at[h, t], pp_r.at[h, t], mate)

    def p_copy(h, t, slot):
        return ctx_copy(
            snd.at[h, same_core(t)], rcv.at[h, slot], p_s.at[h, t], p_r.at[h, slot], same_core(t))

    def c_copy(h, d):
        return ctx_copy(dkvc.at[h, me], dkvc.at[h, me], c_s.at[h, d], c_r.at[h, me], d)

    def c_pass(h, t):
        k = same_core(t)
        return ctx_copy(dkvc.at[h, k], dkvc.at[h, k], c_f.at[h, t], c_r.at[h, k], mate)

    def c_wait(h, k):
        ctx_copy(dkvc.at[h, k], dkvc.at[h, k], c_s.at[h, k], c_r.at[h, k], mate).wait_recv()

    def z_half(h, d, slot):
        return z_copy(dkvz.at[h, slot], dkvz.at[h, slot], z_s.at[h, d], z_r.at[h, slot], d)

    def sc_copy(d, slot):
        return ctx_copy(sqc.at[slot], sqc.at[slot], sc_s.at[d], sc_r.at[slot], d)

    def sz_copy(d, slot):
        return z_copy(sqz.at[slot], sqz.at[slot], sz_s.at[d], sz_r.at[slot], d)

    barrier = pltpu.get_barrier_semaphore()
    each(C, me, lambda d: pl.semaphore_signal(
        barrier, inc=1, device_id={"ctx": d}, device_id_type=pl.DeviceIdType.MESH))
    each(Z, mz, lambda d: pl.semaphore_signal(
        barrier, inc=1, device_id={"kvh": d}, device_id_type=pl.DeviceIdType.MESH))
    own_x = pltpu.make_async_copy(x_cols(me), xall.at[me], loc.at[0])
    own_w = pltpu.make_async_copy(w_rows(mz), wall.at[mz, core], loc.at[1])
    own_x.start()
    own_w.start()

    for h in range(kvd):
        cols = slice(h * 2 * HD, (h + 1) * 2 * HD)
        kvw[h, me] = dot(x_ref[...], w_ref[:, cols], NN).astype(BF16)
        if h == 0:
            pl.semaphore_wait(barrier, C + Z - 2)
        kv_copy(h, mate).start()
        each(chips, chip, lambda t: kv_copy(h, same_core(t)).start(), back=True)
    each(Z, mz, lambda d: w_copy(d, mz).start())
    lse2[...] = lse_ref[...] * math.log2(math.e)

    def reduce(h):
        def add(j, total_sum):
            t = lax.rem(chip + j, chips)
            p_copy(h, t, t).wait_recv()
            return total_sum + rcv[h, t].astype(F32)

        half = lax.fori_loop(1, chips, add, snd[h, me].astype(F32)).astype(BF16)
        dkvc[h, me] = half
        dkvz[h, mz] = half
        each(Z, mz, lambda d: z_half(h, d, mz).start())
        c_copy(h, mate).start()
        each(chips, chip, lambda t: c_copy(h, same_core(t)).start())

    dqacc[...] = jnp.zeros_like(dqacc)
    for h in range(kvd):

        def turn(l, carry):
            for g in range(G):
                hh = h * G + g
                cols = slice(hh * HD, (hh + 1) * HD)
                qt[l, g] = jnp.transpose(q_ref[l, :, cols])
                ot[l, g] = jnp.transpose(o_ref[l, :, cols])
            return carry

        lax.fori_loop(0, L, turn, 0)
        shift = 1 if (h == kvd - 1 and h > 0) else 0

        def step(s, carry):
            t = lax.rem(chip + s // 2 + shift, chips)
            first = lax.rem(s, 2) == 0
            owner = t * 2 + jnp.where(first, 1 - core, core)

            if shift:

                @pl.when(s == 0)
                def _():
                    kv_wait(h, same_core(t))
                    kv_pass(h, t).start()

            @pl.when(first)
            def _():
                kv_wait(h, owner)

            after = lax.rem(t + 1, chips)

            @pl.when(jnp.logical_not(first) & (after != chip) & (s < C - 1))
            def _():
                kv_wait(h, same_core(after))
                kv_pass(h, after).start()

            kmat = kvw[h, owner, :, :HD]
            vmat = kvw[h, owner, :, HD:]
            for kb in range(kper):
                at = owner * own + kb * KBLK
                gap = at + lax.broadcasted_iota(jnp.int32, (QBLK, KBLK), 1)
                gap = gap - lax.broadcasted_iota(jnp.int32, (QBLK, KBLK), 0)
                for qb in range(nq // QBLK):
                    open_block = mask_ref[qb, owner * kper + kb] == 1
                    limit = jnp.where(open_block, off_ref[0] + qb * QBLK, -(1 << 30))
                    bias[qb * QBLK:(qb + 1) * QBLK, kb * KBLK:(kb + 1) * KBLK] = jnp.where(
                        gap < limit, 0.0, -jnp.inf)
            acc[...] = jnp.zeros_like(acc)

            def layer(l, carry):
                for g in range(G):
                    hh = h * G + g
                    cols = slice(hh * HD, (hh + 1) * HD)
                    q = q_ref[l, :, cols]
                    o = o_ref[l, :, cols]
                    sc = dot(q, kmat, NT)
                    pr = jnp.exp2(sc * c2 - lse2[l, :, hh:hh + 1] + bias[...])
                    dp = dot(o, vmat, NT)
                    ds = (pr * (dp - delta_ref[l, :, hh:hh + 1])).astype(BF16)
                    ph = pr.astype(BF16)
                    dqacc[l, hh] += dot(ds, kmat, NN)
                    acc[0] += dot(qt[l, g], ds, NN)
                    acc[1] += dot(ot[l, g], ph, NN)
                return carry

            for l in range(L):
                layer(l, 0)
            snd[h, owner, :, :HD] = jnp.transpose(acc[0] * scale).astype(BF16)
            snd[h, owner, :, HD:] = jnp.transpose(acc[1]).astype(BF16)

            @pl.when(first)
            def _():
                pp_copy(h, t).start()

            @pl.when(jnp.logical_not(first))
            def _():
                pp_copy(h, t).wait_recv()
                both = snd[h, owner].astype(F32) + prt[h, t].astype(F32)
                snd[h, owner] = both.astype(BF16)

                @pl.when(t != chip)
                def _():
                    p_copy(h, t, chip).start()

            if h == 0:

                @pl.when(s == min(2, C - 1))
                def _():
                    each(C, me, lambda d: x_copy(d, me).start())

            if h == kvd - 1:

                @pl.when(s == C - 1)
                def _():
                    own_w.wait()
                    w_pass(mz, core).start()

                    def pass_on(d):
                        w_copy(d, d).wait_recv()
                        w_pass(d, core).start()

                    each(Z, mz, pass_on)

            if h > 0:

                @pl.when(s == min(1, C - 1))
                def _():
                    reduce(h - 1)

            return carry

        lax.fori_loop(0, C, step, 0)

    reduce(kvd - 1)

    def finish(l, carry):
        for hh in range(kvd * G):
            dq_ref[l, :, hh * HD:(hh + 1) * HD] = (dqacc[l, hh] * scale).astype(BF16)
        return carry

    lax.fori_loop(0, L, finish, 0)
    own_x.wait()
    each(C, me, lambda d: x_copy(d, d).wait_recv())

    for h in range(kvd):

        def gather(j, carry):
            t = lax.rem(chip + j, chips)
            c_wait(h, same_core(t))
            c_pass(h, t).start()
            return carry

        lax.fori_loop(1, chips, gather, 0)
    for h in range(kvd):
        each(chips, chip, lambda t: c_wait(h, t * 2 + 1 - core))
        c_wait(h, mate)
    x_all = xall[...].reshape(C * own, cw)
    dkv_all = jnp.concatenate([dkvc[h].reshape(C * own, 2 * HD) for h in range(kvd)], axis=1)
    dw_ref[...] = dot(x_all, dkv_all, TN)
    g = dw_ref[...]
    sqc[me] = jnp.broadcast_to(jnp.sum(g * g, axis=(0, 1), keepdims=True), sqc.shape[1:])
    each(C, me, lambda d: sc_copy(d, me).start())

    w_pass(mz, 1 - core).wait_recv()
    each(Z, mz, lambda d: w_pass(d, 1 - core).wait_recv())
    each(C, me, lambda d: sc_copy(d, d).wait_recv())
    sqz[mz] = jnp.sum(sqc[...], axis=0)
    each(Z, mz, lambda d: sz_copy(d, mz).start())
    for h in range(kvd):
        each(Z, mz, lambda d: z_half(h, d, d).wait_recv())
    dkv_z = jnp.concatenate([dkvz[h, d] for d in range(Z) for h in range(kvd)], axis=1)
    dx = []
    for k in range(2):
        w_all = jnp.concatenate([wall[d, k] for d in range(Z)], axis=1)
        dx.append(dot(dkv_z, w_all, NT))
    dx_ref[...] = jnp.concatenate(dx, axis=1).astype(BF16)

    each(Z, mz, lambda d: sz_copy(d, d).wait_recv())
    msq = jnp.sum(sqz[...], axis=0)[:1, :1] / total
    inv = 1.0 / jnp.sqrt(msq + 1e-6)
    dw_ref[...] = dw_ref[...] * inv

    def drain_chip(t):
        for h in range(kvd):
            kv_copy(h, same_core(t)).wait_send()
            kv_pass(h, t).wait_send()
            p_copy(h, t, chip).wait_send()
            pp_copy(h, t).wait_send()
            c_copy(h, same_core(t)).wait_send()
            c_pass(h, t).wait_send()

    def drain_ctx(d):
        x_copy(d, me).wait_send()
        sc_copy(d, me).wait_send()

    def drain_z(d):
        for h in range(kvd):
            z_half(h, d, mz).wait_send()
        w_copy(d, mz).wait_send()
        w_pass(d, core).wait_send()
        sz_copy(d, mz).wait_send()

    for h in range(kvd):
        kv_copy(h, mate).wait_send()
        pp_copy(h, chip).wait_send()
        c_copy(h, mate).wait_send()
    w_pass(mz, core).wait_send()
    each(chips, chip, drain_chip)
    each(C, me, drain_ctx)
    each(Z, mz, drain_z)


def body(x_kv, w_kv, queries, d_out, lse, delta, offsets, block_mask):
    L, nq, width = queries.shape
    C, Z = lax.axis_size("ctx"), lax.axis_size("kvh")
    own, dm = x_kv.shape
    kvd = w_kv.shape[1] // (2 * HD)
    heads = width // HD
    G = heads // kvd
    cw, zw = dm // C, dm // Z
    if cw % 128 == 0:
        xs = jnp.zeros((8, 128), BF16)
    else:
        xs = jnp.transpose(x_kv.reshape(own, C, cw), (1, 0, 2))
    total = float(dm) * Z * kvd * 2 * HD
    dims = (C, Z, kvd, G, L, nq, own, total)
    vm = pl.BlockSpec(memory_space=pltpu.VMEM)
    blk = (own, 2 * HD)
    dma = pltpu.SemaphoreType.DMA
    flops = 2 * L * heads * nq * own * C * HD * 5
    return pl.pallas_call(
        functools.partial(kernel, dims),
        out_shape=(
            jax.ShapeDtypeStruct(queries.shape, BF16),
            jax.ShapeDtypeStruct((own, zw), BF16),
            jax.ShapeDtypeStruct((cw, kvd * 2 * HD), F32),
        ),
        in_specs=[vm] * 7 + [pl.BlockSpec(memory_space=pltpu.SMEM)] * 2,
        out_specs=(vm, vm, vm),
        scratch_shapes=[
            pltpu.VMEM((kvd, C) + blk, BF16),
            pltpu.VMEM((C, own, cw), BF16),
            pltpu.VMEM((Z, 2, zw // 2, kvd * 2 * HD), BF16),
            pltpu.VMEM((kvd, C) + blk, BF16),
            pltpu.VMEM((kvd, C // 2) + blk, BF16),
            pltpu.VMEM((kvd, C // 2) + blk, BF16),
            pltpu.VMEM((kvd, C) + blk, BF16),
            pltpu.VMEM((kvd, Z) + blk, BF16),
            pltpu.VMEM((L, G, HD, nq), BF16),
            pltpu.VMEM((L, G, HD, nq), BF16),
            pltpu.VMEM(lse.shape, F32),
            pltpu.VMEM((L, heads, nq, HD), F32),
            pltpu.VMEM((nq, own), F32),
            pltpu.VMEM((2, HD, own), F32),
            pltpu.VMEM((C, 8, 128), F32),
            pltpu.VMEM((Z, 8, 128), F32),
            dma((kvd, C)), dma((kvd, C // 2)), dma((kvd, C)),
            dma((C,)), dma((C,)),
            dma((Z,)), dma((Z,)),
            dma((Z,)), dma((Z,)),
            dma((kvd, C // 2)), dma((kvd, C // 2)),
            dma((kvd, C // 2)), dma((kvd, C // 2)),
            dma((kvd, C)), dma((kvd, C // 2)), dma((kvd, C)),
            dma((kvd, Z)), dma((kvd, Z)),
            dma((C,)), dma((C,)),
            dma((Z,)), dma((Z,)),
            dma((2,)),
        ],
        compiler_params=pltpu.CompilerParams(
            collective_id=0, has_side_effects=True, vmem_limit_bytes=60 * 1024 * 1024
        ),
        cost_estimate=pl.CostEstimate(flops=flops, bytes_accessed=1 << 24, transcendentals=0),
    )(x_kv, xs, w_kv, queries, d_out, lse, delta, block_mask, offsets)


def solution(mesh):
    in_specs = (
        P("ctx", None),
        P(None, "kvh"),
        P(None, "ctx", "kvh"),
        P(None, "ctx", "kvh"),
        P(None, "ctx", "kvh"),
        P(None, "ctx", "kvh"),
        P("ctx"),
        P("ctx", None),
    )
    out_specs = (P(None, "ctx", "kvh"), P("ctx", "kvh"), P("ctx", "kvh"))
    return jax.shard_map(body, mesh=mesh, in_specs=in_specs, out_specs=out_specs, check_vma=False)
```
